32 devices in a mesh: grp: 2 (over x), pos: 8 (over z, y), slc: 2 (over core).
Axes of the slice: x: 2, y: 2, z: 4, core: 2. Of those that a mesh axis runs over, the one named last changes fastest.
Arguments:
- object_slices: float32 [4, 2, 1024, 2048], P(('grp', 'slc'), None, 'pos'), parts along dimension 0, may hold values from -4 to 4
- previous: float32 [4, 2, 1024, 2048], P(('grp', 'slc'), None, 'pos'), parts along dimension 0, may hold values from -4 to 4
- probe_modes: bfloat16 [8, 256, 512], P('grp'), parts along dimension 0, may hold values from -4 to 4
- measured: float32 [16, 256, 256], P(('grp', 'pos')), parts along dimension 0, may hold values from 0.2 to 2
- offsets: int32 [16, 2], P(('grp', 'pos')), parts along dimension 0, may hold values from 0 to 1792, as said below
Outputs:
- updated_object: float32 [4, 2, 1024, 2048], P(('grp', 'slc'), None, 'pos'), parts along dimension 0
The draws below stay inside these ranges and needn't reach their ends.
There are 2 independent parts, one for each index of `grp`. The reference program is written for one: setup_inputs(seed, part) draws one part's arguments, and reference() takes and returns one part's arrays. A program takes and returns all parts, laid end to end along the dimension named above; each array names one. Nothing has to cross between parts.
Inputs may be any that keep to these rules, and one draw needn't show every extreme that they name: Each row holds a row offset then a column offset. The row offset of a position in block k of 1 consecutive positions (k from 0) lies within k * 128 - 128 to k * 128; row offsets lie within 0 to 768 and column offsets within 0 to 1792.
All inputs are finite; a program needn't handle non-finite values.
Results may differ from the reference program's by a relative error of at most 0.013.
Values may be sent and summed in bfloat16 or wider, within the bound.
No kernel may reach another device: no remote copies, remote signals or barrier semaphores. Data moves between devices by JAX's collectives and lax.ppermute only.
A program may use at most 64 MiB of HBM per device.

```python
import math
import jax
import jax.numpy as jnp
from jax import lax

W = 256
MODES = 4
P_DEV = 1
COLS = 2048
ROW_DEV = 128
ROWS = 1024
SLICES = 2
POSITIONS = 8


def draw_offsets(key, part):
    row_key = jax.random.fold_in(key, 11)
    column_key = jax.random.fold_in(key, 12)
    block_index = jnp.arange(POSITIONS, dtype=jnp.int32) // P_DEV
    row_starts = block_index * ROW_DEV - ROW_DEV + jax.random.randint(row_key, (POSITIONS,), 0, ROW_DEV + 1, dtype=jnp.int32)
    row_starts = jnp.clip(row_starts, 0, ROWS - W)
    column_starts = jax.random.randint(column_key, (POSITIONS,), 0, COLS - W + 1, dtype=jnp.int32)
    column_starts = column_starts.at[0].set(0).at[POSITIONS - 1].set(COLS - W)
    return jnp.stack([row_starts, column_starts], 1).astype(jnp.int32)


def shard_levels(key, shape, split, least, largest):
    gain, own = 1.0, jax.random.fold_in(key, 6)
    for axis_at, blocks in split:
        draws = jnp.exp(jax.random.uniform(jax.random.fold_in(own, axis_at), (blocks,), jnp.float32, least / len(split), largest / len(split)))
        gain = gain * jnp.repeat(draws, shape[axis_at] // blocks).reshape([-1 if axis == axis_at else 1 for axis in range(len(shape))])
    return gain


def noise(stream_key, dims, scale, bound, shards=(), held_as=jnp.bfloat16):
    values = jax.random.normal(stream_key, dims, jnp.float32) * scale
    if len(shards) > 0:
        values = shard_levels(stream_key, dims, shards, -0.22, 0.18) * values
    return jnp.clip(values, min=-bound, max=bound).astype(held_as)


def setup_inputs(seed: int = 0, part: int = 0) -> dict:
    streams_of = jax.random.split(jax.random.key(seed), 6)
    own_keys = jax.random.split(jax.random.fold_in(streams_of[5], part), 6)
    return {
        "object_slices": noise(own_keys[0], (SLICES, 2, ROWS, COLS), 0.7, 4.0, ((0, 2), (2, 8)), jnp.float32),
        "previous": noise(own_keys[1], (SLICES, 2, ROWS, COLS), 0.7, 4.0, ((0, 2), (2, 8)), jnp.float32),
        "probe_modes": noise(own_keys[2], (MODES, W, 2 * W), 0.5, 4.0),
        "measured": jnp.clip(jnp.exp(math.log(2.0) - 2.3025851 * jax.random.uniform(own_keys[3], (POSITIONS, W, W), jnp.float32) ** shard_levels(own_keys[3], (POSITIONS, W, W), ((0, 8),), -0.2, 0.2)), 0.2, 2.0),
        "offsets": draw_offsets(jax.random.fold_in(jax.random.fold_in(streams_of[5], part), 71), part),
    }


MOMENTUM = 0.5
STEP_SIZE = 0.5
THRESHOLD = 0.1
EPSILON = 0.001

def dft_tables(wave_side, direction):
    indices = jnp.arange(wave_side, dtype=jnp.int32)
    phase_turns = indices[:, None] * indices[None, :] % wave_side
    angles = phase_turns.astype(jnp.float32) * (2.0 * math.pi / wave_side)
    scaling = 1.0 / math.sqrt(wave_side)
    real_part = (jnp.cos(angles) * scaling).astype(jnp.bfloat16)
    imag_part = (direction * jnp.sin(angles) * scaling).astype(jnp.bfloat16)
    return (real_part, imag_part)

def phase_kernel(wave_side):
    indices = jnp.arange(wave_side, dtype=jnp.int32)
    signed = jnp.where(indices < wave_side // 2, indices, indices - wave_side)
    squares = (signed[:, None] * signed[:, None] + signed[None, :] * signed[None, :]) % (2 * wave_side)
    phases = squares.astype(jnp.float32) * (math.pi / wave_side)
    return (jnp.cos(phases), -jnp.sin(phases))

def transform(wave_batch, tables):
    real_part = tables[0].astype(jnp.float32)
    imag_part = tables[1].astype(jnp.float32)
    wave_side = real_part.shape[0]
    stacked = jnp.concatenate([jnp.concatenate([real_part, imag_part], 1), jnp.concatenate([-imag_part, real_part], 1)], 0)
    rounded = lax.optimization_barrier(wave_batch.astype(jnp.bfloat16)).astype(jnp.float32)
    halfway = jnp.einsum('...jk,kl->...jl', rounded, stacked, precision=lax.Precision.HIGHEST)
    halfway = lax.optimization_barrier(halfway.astype(jnp.bfloat16)).astype(jnp.float32)
    half_real = halfway[..., :wave_side]
    half_imag = halfway[..., wave_side:]

    def apply_left(table, operand):
        return jnp.einsum('jk,...kl->...jl', table, operand, precision=lax.Precision.HIGHEST)
    out_real = apply_left(real_part, half_real) - apply_left(imag_part, half_imag)
    out_imag = apply_left(real_part, half_imag) + apply_left(imag_part, half_real)
    return jnp.concatenate([out_real, out_imag], -1)

def complex_product(left_factor, right_factor, conjugate):
    half_side = left_factor.shape[-1] // 2
    left_real = left_factor[..., :half_side]
    left_imag = left_factor[..., half_side:]
    if conjugate:
        left_imag = -left_imag
    right_real = right_factor[..., :half_side]
    right_imag = right_factor[..., half_side:]
    return jnp.concatenate([left_real * right_real - left_imag * right_imag, left_real * right_imag + left_imag * right_real], -1)

def propagate(wave_batch, operators, adjoint):
    forward, inverse, kernel = operators
    kernel_real, kernel_imag = kernel
    if adjoint:
        kernel_imag = -kernel_imag
    spectrum = transform(wave_batch, forward)
    filtered = complex_product(spectrum, jnp.concatenate([kernel_real, kernel_imag], -1), False)
    return transform(filtered, inverse)

def far_adjoint(wave_batch, measured_amp, operators):
    forward, inverse, kernel = operators
    spectrum = transform(wave_batch, forward)
    half_side = spectrum.shape[-1] // 2
    intensity = lax.optimization_barrier(jnp.sum(spectrum[..., :half_side] ** 2 + spectrum[..., half_side:] ** 2, axis=-3))
    amplitude_ratio = 1.0 - measured_amp / jnp.sqrt(intensity + EPSILON)
    weighted = spectrum * jnp.concatenate([amplitude_ratio, amplitude_ratio], -1)[..., None, :, :]
    return transform(weighted, inverse).astype(jnp.bfloat16)

def chain_gradients(probe_modes, windows, measured_amp, operators):
    wave_batch = probe_modes
    saved_waves = []
    for depth_index in range(windows.shape[0]):
        saved_waves.append(wave_batch)
        passed = complex_product(wave_batch.astype(jnp.float32), windows[depth_index].astype(jnp.float32), False)
        wave_batch = propagate(passed, operators, False).astype(jnp.bfloat16)
    adjoints = far_adjoint(wave_batch, measured_amp, operators)
    gradients = [None] * windows.shape[0]
    for depth_index in reversed(range(windows.shape[0])):
        incoming = propagate(adjoints, operators, True)
        gradients[depth_index] = lax.optimization_barrier(jnp.sum(complex_product(saved_waves[depth_index].astype(jnp.float32), incoming, True), axis=-3))
        adjoints = complex_product(windows[depth_index].astype(jnp.float32), incoming, True).astype(jnp.bfloat16)
    return jnp.stack(gradients, 0)

def reference(object_slices, previous, probe_modes, measured, offsets):
    operators = (dft_tables(W, -1.0), dft_tables(W, 1.0), phase_kernel(W))
    extrapolated = object_slices + MOMENTUM * (object_slices - previous)
    rounded = extrapolated.astype(jnp.bfloat16)
    row_starts = offsets[:, 0].astype(jnp.int32)
    column_starts = offsets[:, 1].astype(jnp.int32)

    def one_position(inputs):
        row_start, column_start, measured_amp = inputs
        zero_index = jnp.zeros((), jnp.int32)
        windows = lax.dynamic_slice(rounded, (zero_index, zero_index, row_start, column_start), (SLICES, 2, W, W))
        windows = jnp.concatenate([windows[:, 0], windows[:, 1]], -1)
        return chain_gradients(probe_modes, windows, measured_amp, operators)
    window_grads = lax.map(one_position, (row_starts, column_starts, measured))

    def add_one(index_value, running_sum):
        flat_piece = window_grads[index_value]
        piece = jnp.stack([flat_piece[..., :W], flat_piece[..., W:]], 1)
        zero_index = jnp.zeros((), jnp.int32)
        start = (zero_index, zero_index, row_starts[index_value].astype(jnp.int32), column_starts[index_value].astype(jnp.int32))
        current = lax.dynamic_slice(running_sum, start, piece.shape)
        return lax.dynamic_update_slice(running_sum, current + piece, start)
    gradient = lax.fori_loop(0, POSITIONS, add_one, jnp.zeros(object_slices.shape, jnp.float32))
    stepped = extrapolated - STEP_SIZE * gradient
    return stepped - jnp.clip(stepped, -THRESHOLD, THRESHOLD)
```

```python
import functools
import math

import jax
import jax.numpy as jnp
import ml_dtypes
import numpy as np
from jax import lax
from jax.experimental import pallas as pl
from jax.experimental.pallas import tpu as pltpu
from jax.sharding import PartitionSpec as P

MOMENTUM = 0.5
STEP_SIZE = 0.5
THRESHOLD = 0.1
EPSILON = 0.001
LANES = 128
SUBLANES = 8
BF16 = jnp.bfloat16
F32 = jnp.float32


def bf16_round(values):
    return values.astype(np.float32).astype(ml_dtypes.bfloat16).astype(np.float64)


def chain_tables(side):
    at = np.arange(side)
    angles = (at[:, None] * at[None, :] % side) * (2.0 * math.pi / side)
    scale = 1.0 / math.sqrt(side)
    cosines = bf16_round(np.cos(angles) * scale)
    sines = bf16_round(np.sin(angles) * scale)
    forward, inverse = cosines - 1j * sines, cosines + 1j * sines
    signed = np.where(at < side // 2, at, at - side)
    phase = np.exp(-1j * math.pi * (signed * signed % (2 * side)) / side)
    step = (inverse * phase[None, :]) @ forward
    last = forward @ step

    def real_form(m):
        return np.block([[m.real, -m.imag], [m.imag, m.real]]).astype(np.float32).astype(ml_dtypes.bfloat16)

    a, b = real_form(step), real_form(last)
    return np.stack([a, a.T, b, b.T])


def swap_routes(count):
    first = [(i, i ^ 1) for i in range(count) if i ^ 1 < count]
    second = [(i, j) for i in range(count) for j in (i + 1 if i % 2 else i - 1,) if 0 <= j < count]
    return first, second


def column_base(column, columns, side):
    base = jnp.minimum(column // LANES * LANES, columns - side - LANES)
    return pl.multiple_of(base, LANES), column - base


def shift_out(strip, shift):
    blocks = strip.shape[1] // LANES
    lane = lax.broadcasted_iota(jnp.int32, (strip.shape[0], LANES), 1)
    turn = lax.rem(LANES - shift, LANES)
    rolled = [pltpu.roll(strip[:, j * LANES : (j + 1) * LANES], turn, 1) for j in range(blocks)]
    keep = lane < LANES - shift
    return jnp.concatenate([jnp.where(keep, rolled[j], rolled[j + 1]) for j in range(blocks - 1)], 1)


def shift_in(piece, shift):
    blocks = piece.shape[1] // LANES
    lane = lax.broadcasted_iota(jnp.int32, (piece.shape[0], LANES), 1)
    turn = lax.rem(shift, LANES)
    rolled = [pltpu.roll(piece[:, j * LANES : (j + 1) * LANES], turn, 1) for j in range(blocks)]
    zero = jnp.zeros_like(rolled[0])
    rolled = [zero] + rolled + [zero]
    keep = lane >= shift
    return jnp.concatenate([jnp.where(keep, rolled[j + 1], rolled[j]) for j in range(blocks + 1)], 1)


def rows_out(strip, shift):
    groups = strip.reshape(-1, SUBLANES, strip.shape[1])
    rolled = pltpu.roll(groups, lax.rem(SUBLANES - shift, SUBLANES), 1)
    keep = lax.broadcasted_iota(jnp.int32, (1, SUBLANES, strip.shape[1]), 1) < SUBLANES - shift
    return jnp.where(keep, rolled[:-1], rolled[1:]).reshape(-1, strip.shape[1])


def rows_in(piece, shift):
    groups = piece.reshape(-1, SUBLANES, piece.shape[1])
    rolled = pltpu.roll(groups, shift, 1)
    zero = jnp.zeros_like(rolled[:1])
    keep = lax.broadcasted_iota(jnp.int32, (1, SUBLANES, piece.shape[1]), 1) >= shift
    placed = jnp.where(keep, jnp.concatenate([rolled, zero], 0), jnp.concatenate([zero, rolled], 0))
    return placed.reshape(-1, piece.shape[1])


def cut_kernel(side, offs_ref, offs1_ref, offs2_ref, obj_ref, prv_ref, own_ref, one_ref, two_ref, obj_s, prv_s, sems):
    columns = obj_ref.shape[-1]
    copies, shifts = [], []
    for t, ref in enumerate((offs1_ref, offs2_ref, offs_ref)):
        base, shift = column_base(jnp.clip(ref[0, 1], 0, columns - side), columns, side)
        shifts.append(shift)
        pair = [
            pltpu.make_async_copy(src.at[0, :, :, pl.ds(base, side + LANES)], dst.at[t], sems.at[t, n])
            for n, (src, dst) in enumerate(((obj_ref, obj_s), (prv_ref, prv_s)))
        ]
        for copy in pair:
            copy.start()
        copies.append(pair)
    for t, ref in enumerate((one_ref, two_ref, own_ref)):
        for copy in copies[t]:
            copy.wait()
        for part in range(2):
            now = obj_s[t, part]
            strip = now + MOMENTUM * (now - prv_s[t, part])
            ref[part] = shift_out(strip, shifts[t]).astype(BF16)


def chain_kernel(
    offs_ref, own_ref, own_other_ref, one_ref, one_other_ref, two_ref, two_other_ref, probe_ref, measured_ref, tables_ref,
    g_own_ref, g_one_ref, g_two_ref, band, windows, wave, half, psi, spectrum, grad, gband,
):
    rows = own_ref.shape[1]
    modes, side, _ = probe_ref.shape
    mine = lax.axis_index("slc")
    place = lax.axis_index("pos")
    odd = lax.rem(place, 2)
    start = jnp.clip(offs_ref[0, 0] - (place - 1) * rows, 0, rows)
    at_one = pl.multiple_of((1 - odd) * 2 * rows, rows)
    at_two = pl.multiple_of(odd * 2 * rows, rows)
    for slot, (own, one, two) in ((mine, (own_ref, one_ref, two_ref)), (1 - mine, (own_other_ref, one_other_ref, two_other_ref))):
        band[slot, :, pl.ds(rows, rows)] = own[...].astype(F32)
        band[slot, :, pl.ds(at_one, rows)] = one[...].astype(F32)
        band[slot, :, pl.ds(at_two, rows)] = two[...].astype(F32)

    base = pl.multiple_of(start // SUBLANES * SUBLANES, SUBLANES)
    for s in range(2):
        for part in range(2):
            windows[s, part] = rows_out(band[s, part, pl.ds(base, side + SUBLANES), :], start - base)

    def window(s):
        return windows[s, 0], windows[s, 1]

    def sandwich(right, left, out):
        h = jnp.dot(wave[...].reshape(modes * side, 2 * side), tables_ref[right], preferred_element_type=F32).astype(BF16)
        half[...] = h.reshape(modes, side, 2 * side)
        for m in range(modes):
            stacked = jnp.concatenate([half[m, :, :side], half[m, :, side:]], 0)
            out(m, jnp.dot(tables_ref[left], stacked, preferred_element_type=F32))

    def put_wave(m, real, imag):
        wave[m, :, :side] = real.astype(BF16)
        wave[m, :, side:] = imag.astype(BF16)

    o_real, o_imag = window(0)
    for m in range(modes):
        p_real, p_imag = probe_ref[m, :, :side].astype(F32), probe_ref[m, :, side:].astype(F32)
        put_wave(m, p_real * o_real - p_imag * o_imag, p_real * o_imag + p_imag * o_real)

    def after_first(m, out):
        psi[m] = out.astype(BF16)

    sandwich(1, 0, after_first)
    o_real, o_imag = window(1)
    for m in range(modes):
        p_real, p_imag = psi[m, :side].astype(F32), psi[m, side:].astype(F32)
        put_wave(m, p_real * o_real - p_imag * o_imag, p_real * o_imag + p_imag * o_real)

    def after_last(m, out):
        spectrum[m] = out

    sandwich(3, 2, after_last)
    intensity = jnp.zeros((side, side), F32)
    for m in range(modes):
        intensity += spectrum[m, :side] ** 2 + spectrum[m, side:] ** 2
    ratio = 1.0 - measured_ref[0] / jnp.sqrt(intensity + EPSILON)
    for m in range(modes):
        put_wave(m, ratio * spectrum[m, :side], ratio * spectrum[m, side:])

    grad[...] = jnp.zeros_like(grad)

    def after_back_last(m, u):
        u_real, u_imag = u[:side], u[side:]
        p_real, p_imag = psi[m, :side].astype(F32), psi[m, side:].astype(F32)
        grad[0] += p_real * u_real + p_imag * u_imag
        grad[1] += p_real * u_imag - p_imag * u_real
        o_real, o_imag = window(1)
        put_wave(m, o_real * u_real + o_imag * u_imag, o_real * u_imag - o_imag * u_real)

    sandwich(2, 3, after_back_last)

    @pl.when(mine == 0)
    def _():
        grad[...] = jnp.zeros_like(grad)

        def after_back_first(m, u):
            u_real, u_imag = u[:side], u[side:]
            p_real, p_imag = probe_ref[m, :, :side].astype(F32), probe_ref[m, :, side:].astype(F32)
            grad[0] += p_real * u_real + p_imag * u_imag
            grad[1] += p_real * u_imag - p_imag * u_real

        sandwich(0, 1, after_back_first)

    gband[...] = jnp.zeros_like(gband)
    for part in range(2):
        gband[part, pl.ds(base, side + SUBLANES), :] = rows_in(grad[part], start - base)
    g_own_ref[...] = gband[:, pl.ds(rows, rows), :]
    g_one_ref[...] = gband[:, pl.ds(at_one, rows), :].astype(BF16)
    g_two_ref[...] = gband[:, pl.ds(at_two, rows), :].astype(BF16)


def final_kernel(side, offs_ref, offs1_ref, offs2_ref, ext_ref, own_ref, one_ref, two_ref, out_ref, total):
    columns = ext_ref.shape[-1]
    total[...] = jnp.zeros_like(total)
    for ref, piece in ((offs_ref, own_ref), (offs1_ref, one_ref), (offs2_ref, two_ref)):
        base, shift = column_base(jnp.clip(ref[0, 1], 0, columns - side), columns, side)
        for part in range(2):
            total[part, :, pl.ds(base, side + LANES)] += shift_in(piece[part].astype(F32), shift)
    stepped = ext_ref[...] - STEP_SIZE * total[...]
    out_ref[0] = stepped - jnp.clip(stepped, -THRESHOLD, THRESHOLD)


def extrapolate_kernel(obj_ref, prv_ref, ext_ref):
    now = obj_ref[0]
    ext_ref[...] = now + MOMENTUM * (now - prv_ref[0])


SMEM = pl.BlockSpec(memory_space=pltpu.SMEM)
VMEM = pl.BlockSpec(memory_space=pltpu.VMEM)
ANY = pl.BlockSpec(memory_space=pl.ANY)
PARAMS = pltpu.CompilerParams(vmem_limit_bytes=56 * 2**20)


def shards(tables, object_slices, previous, probe_modes, measured, offsets):
    rows, columns = object_slices.shape[2:]
    modes, side, _ = probe_modes.shape
    first, second = swap_routes(lax.axis_size("pos"))
    other = [(0, 1), (1, 0)]
    offs1 = lax.ppermute(offsets, "pos", first)
    offs2 = lax.ppermute(offsets, "pos", second)
    piece = jax.ShapeDtypeStruct((2, rows, side), BF16)
    own, one, two = pl.pallas_call(
        functools.partial(cut_kernel, side),
        out_shape=[piece] * 3,
        in_specs=[SMEM] * 3 + [ANY] * 2,
        out_specs=[VMEM] * 3,
        scratch_shapes=[pltpu.VMEM((3, 2, rows, side + LANES), F32)] * 2 + [pltpu.SemaphoreType.DMA((3, 2))],
        compiler_params=PARAMS,
        name="cut",
    )(offsets, offs1, offs2, object_slices, previous)
    one = lax.ppermute(one, "pos", first)
    two = lax.ppermute(two, "pos", second)
    own_other = lax.ppermute(own, "slc", other)
    one_other = lax.ppermute(one, "slc", other)
    two_other = lax.ppermute(two, "slc", other)
    g_own, g_one, g_two = pl.pallas_call(
        chain_kernel,
        out_shape=[jax.ShapeDtypeStruct((2, rows, side), F32), piece, piece],
        in_specs=[SMEM] + [VMEM] * 9,
        out_specs=[VMEM] * 3,
        scratch_shapes=[
            pltpu.VMEM((2, 2, 3 * rows + SUBLANES, side), F32),
            pltpu.VMEM((2, 2, side, side), F32),
            pltpu.VMEM((modes, side, 2 * side), BF16),
            pltpu.VMEM((modes, side, 2 * side), BF16),
            pltpu.VMEM((modes, 2 * side, side), BF16),
            pltpu.VMEM((modes, 2 * side, side), F32),
            pltpu.VMEM((2, side, side), F32),
            pltpu.VMEM((2, 3 * rows + SUBLANES, side), F32),
        ],
        compiler_params=PARAMS,
        name="chain",
    )(offsets, own, own_other, one, one_other, two, two_other, probe_modes, measured, tables)
    g_one = lax.ppermute(g_one, "pos", first)
    g_two = lax.ppermute(g_two, "pos", second)
    ext = pl.pallas_call(
        extrapolate_kernel,
        out_shape=jax.ShapeDtypeStruct((2, rows, columns), F32),
        in_specs=[VMEM] * 2,
        out_specs=VMEM,
        compiler_params=PARAMS,
        cost_estimate=pl.CostEstimate(flops=2 * 3 * rows * columns, bytes_accessed=24 * rows * columns, transcendentals=0),
        name="extrapolate",
    )(object_slices, previous)
    return pl.pallas_call(
        functools.partial(final_kernel, side),
        out_shape=jax.ShapeDtypeStruct(object_slices.shape, F32),
        in_specs=[SMEM] * 3 + [VMEM] * 4,
        out_specs=VMEM,
        scratch_shapes=[pltpu.VMEM((2, rows, columns), F32)],
        compiler_params=PARAMS,
        name="update",
    )(offsets, offs1, offs2, ext, g_own, g_one, g_two)


def solution(mesh):
    placed = (
        P(("grp", "slc"), None, "pos", None),
        P(("grp", "slc"), None, "pos", None),
        P("grp", None, None),
        P(("grp", "pos"), None, None),
        P(("grp", "pos"), None),
    )

    def run(object_slices, previous, probe_modes, measured, offsets):
        tables = chain_tables(probe_modes.shape[1])
        return jax.shard_map(
            functools.partial(shards, tables),
            mesh=mesh,
            in_specs=placed,
            out_specs=P(("grp", "slc"), None, "pos", None),
            check_vma=False,
        )(object_slices, previous, probe_modes, measured, offsets)

    return run
```
